256 devices in a mesh: row: 64 (over x, z, y_hi), col: 4 (over y_lo, core).
Axes of the slice: x: 4, y: 4 (y_hi: 2, y_lo: 2; y = y_hi * 2 + y_lo), z: 8, core: 2. Of those that a mesh axis runs over, the one named last changes fastest.
Arguments:
- eigvecs: bfloat16 [196608, 3072], P('row', 'col'), may hold values from -6 to 6
- panels: bfloat16 [196608, 512], P('row', 'col'), may hold values from -1 to 1
- t_factors: float32 [2, 256, 256], replicated, may hold values from -1 to 1, as said below
Outputs:
- transformed: bfloat16 [196608, 3072], P('row', 'col')
The draws below stay inside these ranges and needn't reach their ends.
Inputs may be any that keep to these rules, and one draw needn't show every extreme that they name: `t_factors`: each of the two factors is upper triangular with a positive diagonal.
All inputs are finite; a program needn't handle non-finite values.
Results may differ from the reference program's by a relative error of at most 0.0053.
Values may be sent and summed in bfloat16 or wider, within the bound.
A program may use at most 64 MiB of HBM per device.

```python
import jax
import jax.numpy as jnp
from jax import lax

N = 196608
NB = 256
K = 3072


def draw_t_factors(key, part):
    key = jax.random.fold_in(key, 5)
    key_off, key_diag = jax.random.split(key)
    offdiag = jnp.clip(jax.random.normal(key_off, (2, NB, NB), jnp.float32), -4.0, 4.0)
    diagonal = jax.random.uniform(key_diag, (2, NB), jnp.float32, 1.0, 2.0)
    strictly = jnp.triu(jnp.ones((NB, NB), jnp.float32), 1)
    identity = jnp.eye(NB, dtype=jnp.float32)
    scaled_off = strictly * offdiag * (0.5 / jnp.sqrt(jnp.float32(N)))
    scaled_diag = identity * diagonal[:, :, None] * jnp.sqrt(jnp.float32(NB) / jnp.float32(N))
    return scaled_off + scaled_diag


def block_scale(key, dims, pieces, least, largest):
    def one(position, shards_of):
        steps = jax.random.uniform(jax.random.fold_in(jax.random.fold_in(key, 6), position), (shards_of,), jnp.float32, least / len(pieces), largest / len(pieces))
        return jnp.repeat(jnp.exp(steps), dims[position] // shards_of).reshape((-1,) + (1,) * (len(dims) - position - 1))

    factor_of = one(*pieces[0])
    for cut in pieces[1:]:
        factor_of = factor_of * one(*cut)
    return factor_of


def scatter_about(own_key, extent, deviation, limit, cuts=(), kind=jnp.bfloat16):
    entries = deviation * jax.random.normal(own_key, extent, jnp.float32)
    if cuts:
        entries = entries * block_scale(own_key, extent, cuts, -0.22, 0.18)
    return jnp.clip(entries, -limit, limit).astype(kind)


def setup_inputs(seed: int = 0) -> dict:
    streams_of = jax.random.split(jax.random.key(seed), 4)
    return {
        "eigvecs": scatter_about(streams_of[0], (N, K), 1.0, 6.0, ((0, 64), (1, 4))),
        "panels": scatter_about(streams_of[1], (N, 2 * NB), (NB ** -0.5), 1.0, ((0, 64), (1, 4))),
        "t_factors": draw_t_factors(jax.random.fold_in(streams_of[3], 71), 0),
    }


def reference(eigvecs, panels, t_factors):
    leading = panels[:, :NB]
    trailing = panels[:, NB:]
    projected = jnp.einsum("rp,rc->pc", panels, eigvecs, preferred_element_type=jnp.float32)
    coupling = jnp.einsum("rp,rq->pq", trailing, leading, preferred_element_type=jnp.float32)
    y_lead = jnp.dot(t_factors[0], projected[:NB], precision=lax.Precision.HIGHEST).astype(jnp.bfloat16)
    second = projected[NB:] - jnp.dot(coupling, y_lead.astype(jnp.float32), precision=lax.Precision.HIGHEST)
    y_trail = jnp.dot(t_factors[1], second, precision=lax.Precision.HIGHEST).astype(jnp.bfloat16)
    stacked = jnp.concatenate([y_lead, y_trail], axis=0)
    update = jnp.dot(panels, stacked, preferred_element_type=jnp.float32)
    return (eigvecs.astype(jnp.float32) - update).astype(jnp.bfloat16)
```

```python
import functools

import jax
import jax.numpy as jnp
from jax import lax
from jax.experimental import pallas as pl
from jax.experimental.pallas import tpu as pltpu
from jax.sharding import PartitionSpec as P

MESH = pl.DeviceIdType.MESH
NX, NZ = 4, 8
ROWS = 3072
COLS = 768
W = 128
WIDE = COLS + 2 * W
HALF = ROWS // 2
CHUNKS = 3
CHUNK = HALF // CHUNKS
GROUPS = (64, 32, 32)
BF16 = jnp.bfloat16
F32 = jnp.float32


def tdot(a, b):
    return lax.dot_general(a, b, (((0,), (0,)), ((), ())), preferred_element_type=F32)


def dot(a, b):
    return jnp.dot(a, b, preferred_element_type=F32)


def split(value):
    high = value.astype(BF16)
    return high, (value - high.astype(F32)).astype(BF16)


def place():
    row, col = lax.axis_index("row"), lax.axis_index("col")
    return row // 16, lax.rem(row // 2, 8), lax.rem(row, 2), col // 2, lax.rem(col, 2)


def device(x, z, y_hi, y_lo, core):
    return ((x * NZ + z) * 2 + y_hi, y_lo * 2 + core)


class Group:
    def __init__(self, depth, refs):
        self.depth = depth
        (self.acc, self.xs, self.xr, self.zf, self.zs, self.zr, self.yf, self.yr, self.full, self.sem3, self.sem7, self.sem1) = refs

    def bind(self, x, z, y_hi, y_lo, core):
        self.x, self.z = x, z
        self.x_peer = [device(lax.rem(x + d, NX), z, y_hi, y_lo, core) for d in range(1, NX)]
        self.z_peer = [device(x, lax.rem(z + d, NZ), y_hi, y_lo, core) for d in range(1, NZ)]
        self.y_peer = device(x, z, 1 - y_hi, y_lo, core)

    def copy(self, src, dst, send, recv, peer):
        return pltpu.make_async_remote_copy(
            src_ref=src, dst_ref=dst, send_sem=send, recv_sem=recv, device_id=peer, device_id_type=MESH
        )

    def x_reduce(self):
        return [
            self.copy(self.xs.at[lax.rem(self.x + d, NX)], self.xr.at[d - 1], self.sem3.at[0, d - 1], self.sem3.at[1, d - 1], self.x_peer[d - 1])
            for d in range(1, NX)
        ]

    def z_reduce(self):
        return [
            self.copy(self.zs.at[lax.rem(self.z + d, NZ)], self.zr.at[d - 1], self.sem7.at[0, d - 1], self.sem7.at[1, d - 1], self.z_peer[d - 1])
            for d in range(1, NZ)
        ]

    def y_swap(self):
        return self.copy(self.yf, self.yr, self.sem1.at[0], self.sem1.at[1], self.y_peer)

    def z_gather(self, sender):
        out = []
        for d in range(1, NZ):
            block = self.full.at[self.x, self.z if sender else lax.rem(self.z + NZ - d, NZ)]
            out.append(self.copy(block, block, self.sem7.at[2, d - 1], self.sem7.at[3, d - 1], self.z_peer[d - 1]))
        return out

    def x_gather(self, sender):
        out = []
        for d in range(1, NX):
            block = self.full.at[self.x if sender else lax.rem(self.x + NX - d, NX)]
            out.append(self.copy(block, block, self.sem3.at[2, d - 1], self.sem3.at[3, d - 1], self.x_peer[d - 1]))
        return out

    def step1(self):
        self.xs[...] = self.acc[...].astype(BF16)
        for c in self.x_reduce():
            c.start()

    def step2(self):
        for c in self.x_reduce():
            c.wait_recv()
        total = self.acc[self.x]
        for d in range(NX - 1):
            total = total + self.xr[d].astype(F32)
        for t in range(NZ):
            tile = total[:, t * W : (t + 1) * W]
            self.zf[t] = tile
            self.zs[t] = tile.astype(BF16)
        for c in self.z_reduce():
            c.start()

    def step3(self):
        for c in self.z_reduce():
            c.wait_recv()
        total = self.zf[self.z]
        for d in range(NZ - 1):
            total = total + self.zr[d].astype(F32)
        self.yf[...] = total
        self.y_swap().start()

    def step4(self):
        self.y_swap().wait_recv()
        self.full[self.x, self.z] = (self.yf[...] + self.yr[...]).astype(BF16)
        for c in self.z_gather(True):
            c.start()

    def step5(self):
        for c in self.z_gather(False):
            c.wait_recv()
        for c in self.x_gather(True):
            c.start()

    def step6(self):
        for c in self.x_gather(False):
            c.wait_recv()

    def drain(self):
        for c in self.x_reduce() + self.z_reduce() + [self.y_swap()] + self.z_gather(True) + self.x_gather(True):
            c.wait_send()

    def columns(self, first, tiles):
        strips = [jnp.concatenate([self.full[k, t] for k in range(NX)], axis=0) for t in range(first, first + tiles)]
        return jnp.concatenate(strips, axis=1)


def group_scratch(depth):
    return [
        pltpu.VMEM((NX, depth, WIDE), F32),
        pltpu.VMEM((NX, depth, WIDE), BF16),
        pltpu.VMEM((NX - 1, depth, WIDE), BF16),
        pltpu.VMEM((NZ, depth, W), F32),
        pltpu.VMEM((NZ, depth, W), BF16),
        pltpu.VMEM((NZ - 1, depth, W), BF16),
        pltpu.VMEM((depth, W), F32),
        pltpu.VMEM((depth, W), F32),
        pltpu.VMEM((NX, NZ, depth, W), BF16),
        pltpu.SemaphoreType.DMA((4, NX - 1)),
        pltpu.SemaphoreType.DMA((4, NZ - 1)),
        pltpu.SemaphoreType.DMA((2,)),
    ]


PER_GROUP = 12


def gather_and_reduce(e_hbm, p_hbm, t_hbm, e, g, y, t, *scratch):
    groups = [Group(depth, scratch[k * PER_GROUP : (k + 1) * PER_GROUP]) for k, depth in enumerate(GROUPS)]
    load_sem, core_sem, y_sem, fwd_sem = scratch[len(GROUPS) * PER_GROUP :]
    x, z, y_hi, y_lo, core = place()
    for group in groups:
        group.bind(x, z, y_hi, y_lo, core)
    own, other = 2 * y_lo, 2 * (1 - y_lo)
    sibling = device(x, z, y_hi, y_lo, 1 - core)
    partner = device(x, z, y_hi, 1 - y_lo, core)

    load_p = pltpu.make_async_copy(p_hbm, g.at[own + core], load_sem.at[0])
    load_e = pltpu.make_async_copy(e_hbm, e, load_sem.at[1])
    load_t = pltpu.make_async_copy(t_hbm, t, load_sem.at[2])
    load_p.start()
    load_e.start()
    load_t.start()

    barrier = pltpu.get_barrier_semaphore()
    peers = [sibling, partner, groups[0].y_peer] + groups[0].x_peer + groups[0].z_peer
    for peer in peers:
        pl.semaphore_signal(barrier, inc=1, device_id=peer, device_id_type=MESH)
    pl.semaphore_wait(barrier, len(peers))

    def remote(src, dst, send, recv, peer):
        return pltpu.make_async_remote_copy(
            src_ref=src, dst_ref=dst, send_sem=send, recv_sem=recv, device_id=peer, device_id_type=MESH
        )

    def share(part, owner):
        half = (1 - owner) if part == 0 else owner
        block = g.at[own + owner, pl.ds(pl.multiple_of(half * HALF, HALF), HALF)]
        return remote(block, block, core_sem.at[0, part], core_sem.at[1, part], sibling)

    def rows_of(half, k):
        return pl.ds(pl.multiple_of(half * HALF + k * CHUNK, CHUNK), CHUNK)

    def across(first, j, k):
        block = g.at[first + j, rows_of(core, k)]
        return remote(block, block, y_sem.at[0, j, k], y_sem.at[1, j, k], partner)

    def forward(half, j, k):
        block = g.at[other + j, rows_of(half, k)]
        return remote(block, block, fwd_sem.at[0, j, k], fwd_sem.at[1, j, k], sibling)

    load_p.wait()
    share(0, core).start()

    @pl.when(core == 0)
    def _():
        for k in range(CHUNKS):
            across(own, 0, k).start()

    share(1, core).start()
    share(0, 1 - core).wait_recv()

    @pl.when(core == 1)
    def _():
        for k in range(CHUNKS):
            across(own, 0, k).start()

    for k in range(CHUNKS):
        across(own, 1, k).start()

    share(1, 1 - core).wait_recv()
    load_e.wait()

    def wide(rows, tile):
        if tile < 3:
            return e[rows, tile * 256 : (tile + 1) * 256]
        return jnp.concatenate([g[own, rows], g[own + 1, rows]], axis=1)

    def project(group, blocks, rows, start):
        left = jnp.concatenate([g[b, rows] for b in blocks], axis=1) if len(blocks) > 1 else g[blocks[0], rows]
        for tile in range(4):
            part = tdot(left, wide(rows, tile)).reshape(NX, group.depth, 256)
            where = (slice(None), slice(None), slice(tile * 256, (tile + 1) * 256))
            if start:
                group.acc[where] = part
            else:
                group.acc[where] += part

    first, middle, last = groups
    project(first, [own, own + 1], pl.ds(0, CHUNK), True)

    @pl.loop(1, ROWS // CHUNK)
    def _(k):
        project(first, [own, own + 1], pl.ds(pl.multiple_of(k * CHUNK, CHUNK), CHUNK), False)

    first.step1()

    def arrive(j, k, group):
        across(other, j, k).wait_recv()
        forward(core, j, k).start()
        project(group, [other + j], rows_of(core, k), k == 0)
        forward(1 - core, j, k).wait_recv()
        project(group, [other + j], rows_of(1 - core, k), False)

    arrive(0, 0, middle)
    arrive(0, 1, middle)
    first.step2()
    arrive(0, 2, middle)
    middle.step1()
    arrive(1, 0, last)
    first.step3()
    arrive(1, 1, last)
    first.step4()
    middle.step2()
    arrive(1, 2, last)
    last.step1()
    middle.step3()
    first.step5()
    middle.step4()
    last.step2()
    middle.step5()
    last.step3()
    last.step4()
    last.step5()
    load_t.wait()
    t0_high, t0_low = split(t[0])
    t1_high, t1_low = split(t[1])
    first.step6()
    middle.step6()
    last.step6()

    def finish(p1, p2, cross, transposed):
        for n in range(3):
            lead_in = p1(n)
            lead = (dot(t0_high, lead_in) + dot(t0_low, lead_in)).astype(BF16)
            y[0:256, n * 256 : (n + 1) * 256] = lead
            pulled = tdot(cross, lead) if transposed else dot(cross, lead)
            high, low = split(p2(n).astype(F32) - pulled)
            trail = dot(t1_high, high) + dot(t1_high, low) + dot(t1_low, high)
            y[256:512, n * 256 : (n + 1) * 256] = trail.astype(BF16)

    def mine(n):
        return first.columns(2 * n, 2)

    def theirs(n):
        return jnp.concatenate([middle.columns(2 * n, 2), last.columns(2 * n, 2)], axis=0)

    @pl.when(y_lo == 0)
    def _():
        finish(mine, theirs, theirs(3), False)

    @pl.when(y_lo == 1)
    def _():
        finish(theirs, mine, theirs(3), True)

    share(0, core).wait_send()
    share(1, core).wait_send()
    for j in range(2):
        for k in range(CHUNKS):
            across(own, j, k).wait_send()
            forward(core, j, k).wait_send()
    for group in groups:
        group.drain()


BLOCK = 512


def update(e, g, y, out):
    rows = pl.ds(pl.multiple_of(pl.program_id(0) * BLOCK, BLOCK), BLOCK)
    left = jnp.concatenate([g[b, rows] for b in range(4)], axis=1)
    for n in range(3):
        where = slice(n * 256, (n + 1) * 256)
        out[:, where] = (e[rows, where].astype(F32) - dot(left, y[:, where])).astype(BF16)


def per_device(eigvecs, panels, t_factors):
    scratch = [pltpu.VMEM((2, 256, 256), F32)]
    for depth in GROUPS:
        scratch += group_scratch(depth)
    scratch += [
        pltpu.SemaphoreType.DMA((3,)),
        pltpu.SemaphoreType.DMA((2, 2)),
        pltpu.SemaphoreType.DMA((2, 2, CHUNKS)),
        pltpu.SemaphoreType.DMA((2, 2, CHUNKS)),
    ]
    hbm = pl.BlockSpec(memory_space=pltpu.HBM)
    vmem = pl.BlockSpec(memory_space=pltpu.VMEM)
    e, g, y = pl.pallas_call(
        gather_and_reduce,
        out_shape=(
            pltpu.VMEM((ROWS, COLS), BF16),
            pltpu.VMEM((4, ROWS, W), BF16),
            pltpu.VMEM((512, COLS), BF16),
        ),
        in_specs=[hbm] * 3,
        out_specs=(vmem,) * 3,
        scratch_shapes=scratch,
        compiler_params=pltpu.CompilerParams(collective_id=0, has_side_effects=True, vmem_limit_bytes=32 << 20),
        name="gather_and_reduce",
    )(*[pltpu.with_memory_space_constraint(a, pltpu.HBM) for a in (eigvecs, panels, t_factors)])
    return pl.pallas_call(
        update,
        out_shape=jax.ShapeDtypeStruct((ROWS, COLS), BF16),
        grid=(ROWS // BLOCK,),
        in_specs=[vmem] * 3,
        out_specs=pl.BlockSpec((BLOCK, COLS), lambda i: (i, 0)),
        compiler_params=pltpu.CompilerParams(vmem_limit_bytes=24 << 20),
        name="update",
    )(e, g, y)


def solution(mesh):
    in_specs = (P("row", "col"), P("row", "col"), P())
    return jax.shard_map(per_device, mesh=mesh, in_specs=in_specs, out_specs=P("row", "col"), check_vma=False)
```

```python
import jax
import jax.numpy as jnp
from jax import lax
from jax.experimental import pallas as pl
from jax.experimental.pallas import tpu as pltpu
from jax.sharding import PartitionSpec as P

MESH = pl.DeviceIdType.MESH
NX, NZ = 4, 8
ROWS = 3072
COLS = 768
W = 128
WIDE = COLS + 2 * W
HALF = ROWS // 2
CHUNKS = 3
CHUNK = HALF // CHUNKS
DEPTH = 2
GROUPS = ((64, 6), (32, 8), (32, 8))
BF16 = jnp.bfloat16
F32 = jnp.float32


def tdot(a, b):
    return lax.dot_general(a, b, (((0,), (0,)), ((), ())), preferred_element_type=F32)


def dot(a, b):
    return jnp.dot(a, b, preferred_element_type=F32)


def split(value):
    high = value.astype(BF16)
    return high, (value - high.astype(F32)).astype(BF16)


def place():
    row, col = lax.axis_index("row"), lax.axis_index("col")
    return row // 16, lax.rem(row // 2, 8), lax.rem(row, 2), col // 2, lax.rem(col, 2)


def device(x, z, y_hi, y_lo, core):
    return ((x * NZ + z) * 2 + y_hi, y_lo * 2 + core)


class Group:
    def __init__(self, depth, tiles, refs):
        self.depth, self.tiles, self.part = depth, tiles, depth * tiles // NZ
        (self.acc, self.xs, self.xr, self.zf, self.zs, self.zr, self.yf, self.yr, self.full, self.sem3, self.sem7, self.sem1) = refs

    def bind(self, x, z, y_hi, y_lo, core):
        self.x, self.z = x, z
        self.x_peer = [device(lax.rem(x + d, NX), z, y_hi, y_lo, core) for d in range(1, NX)]
        self.z_peer = [device(x, lax.rem(z + d, NZ), y_hi, y_lo, core) for d in range(1, NZ)]
        self.y_peer = device(x, z, 1 - y_hi, y_lo, core)

    def copy(self, src, dst, send, recv, peer):
        return pltpu.make_async_remote_copy(
            src_ref=src, dst_ref=dst, send_sem=send, recv_sem=recv, device_id=peer, device_id_type=MESH
        )

    def slot(self, z):
        return pl.ds(pl.multiple_of(z * self.part, 16), self.part)

    def x_reduce(self):
        return [
            self.copy(self.xs.at[lax.rem(self.x + d, NX)], self.xr.at[d - 1], self.sem3.at[0, d - 1], self.sem3.at[1, d - 1], self.x_peer[d - 1])
            for d in range(1, NX)
        ]

    def z_reduce(self):
        return [
            self.copy(self.zs.at[self.slot(lax.rem(self.z + d, NZ))], self.zr.at[d - 1], self.sem7.at[0, d - 1], self.sem7.at[1, d - 1], self.z_peer[d - 1])
            for d in range(1, NZ)
        ]

    def y_swap(self):
        return self.copy(self.yf, self.yr, self.sem1.at[0], self.sem1.at[1], self.y_peer)

    def z_gather(self, sender):
        out = []
        for d in range(1, NZ):
            block = self.full.at[self.x, self.slot(self.z if sender else lax.rem(self.z + NZ - d, NZ))]
            out.append(self.copy(block, block, self.sem7.at[2, d - 1], self.sem7.at[3, d - 1], self.z_peer[d - 1]))
        return out

    def x_gather(self, sender):
        out = []
        for d in range(1, NX):
            block = self.full.at[self.x if sender else lax.rem(self.x + NX - d, NX)]
            out.append(self.copy(block, block, self.sem3.at[2, d - 1], self.sem3.at[3, d - 1], self.x_peer[d - 1]))
        return out

    def step1(self):
        self.xs[...] = self.acc[...].astype(BF16)
        for c in self.x_reduce():
            c.start()

    def step2(self):
        for c in self.x_reduce():
            c.wait_recv()
        total = self.acc[self.x]
        for d in range(NX - 1):
            total = total + self.xr[d].astype(F32)
        for t in range(self.tiles):
            tile, where = total[:, t * W : (t + 1) * W], slice(t * self.depth, (t + 1) * self.depth)
            self.zf[where] = tile
            self.zs[where] = tile.astype(BF16)
        for c in self.z_reduce():
            c.start()

    def step3(self):
        for c in self.z_reduce():
            c.wait_recv()
        total = self.zf[self.slot(self.z)]
        for d in range(NZ - 1):
            total = total + self.zr[d].astype(F32)
        self.yf[...] = total
        self.y_swap().start()

    def step4(self):
        self.y_swap().wait_recv()
        self.full[self.x, self.slot(self.z)] = (self.yf[...] + self.yr[...]).astype(BF16)
        for c in self.z_gather(True):
            c.start()

    def step5(self, which=None):
        for c in self.z_gather(False):
            c.wait_recv()
        if which is None: which=range(NX-1)
        cs = self.x_gather(True)
        for d in which:
            cs[d].start()

    def step5b(self, which):
        cs = self.x_gather(True)
        for d in which:
            cs[d].start()

    def step6(self):
        for c in self.x_gather(False):
            c.wait_recv()

    def drain(self):
        for c in self.x_reduce() + self.z_reduce() + [self.y_swap()] + self.z_gather(True) + self.x_gather(True):
            c.wait_send()

    def columns(self, first, tiles):
        n = self.depth
        strips = [jnp.concatenate([self.full[k, t * n : (t + 1) * n] for k in range(NX)], axis=0) for t in range(first, first + tiles)]
        return jnp.concatenate(strips, axis=1)


def group_scratch(depth, tiles):
    wide, flat, part = tiles * W, tiles * depth, tiles * depth // NZ
    return [
        pltpu.VMEM((NX, depth, wide), F32),
        pltpu.VMEM((NX, depth, wide), BF16),
        pltpu.VMEM((NX - 1, depth, wide), BF16),
        pltpu.VMEM((flat, W), F32),
        pltpu.VMEM((flat, W), BF16),
        pltpu.VMEM((NZ - 1, part, W), BF16),
        pltpu.VMEM((part, W), F32),
        pltpu.VMEM((part, W), F32),
        pltpu.VMEM((NX, flat, W), BF16),
        pltpu.SemaphoreType.DMA((4, NX - 1)),
        pltpu.SemaphoreType.DMA((4, NZ - 1)),
        pltpu.SemaphoreType.DMA((2,)),
    ]


PER_GROUP = 12


def gather_and_reduce(e_hbm, p_hbm, t_hbm, e, g, y, t, *scratch):
    groups = [Group(*size, scratch[k * PER_GROUP : (k + 1) * PER_GROUP]) for k, size in enumerate(GROUPS)]
    load_sem, core_sem, y_sem, fwd_sem = scratch[len(GROUPS) * PER_GROUP :]
    x, z, y_hi, y_lo, core = place()
    for group in groups:
        group.bind(x, z, y_hi, y_lo, core)
    own, other = 2 * y_lo, 2 * (1 - y_lo)
    sibling = device(x, z, y_hi, y_lo, 1 - core)
    partner = device(x, z, y_hi, 1 - y_lo, core)

    load_p = pltpu.make_async_copy(p_hbm, g.at[own + core], load_sem.at[0])
    load_e = pltpu.make_async_copy(e_hbm, e, load_sem.at[1])
    load_t = pltpu.make_async_copy(t_hbm, t, load_sem.at[2])
    load_p.start()
    load_e.start()
    load_t.start()

    barrier = pltpu.get_barrier_semaphore()
    peers = [sibling, partner, groups[0].y_peer] + groups[0].x_peer + groups[0].z_peer
    for peer in peers:
        pl.semaphore_signal(barrier, inc=1, device_id=peer, device_id_type=MESH)
    pl.semaphore_wait(barrier, len(peers))

    def remote(src, dst, send, recv, peer):
        return pltpu.make_async_remote_copy(
            src_ref=src, dst_ref=dst, send_sem=send, recv_sem=recv, device_id=peer, device_id_type=MESH
        )

    def share(part, owner):
        half = (1 - owner) if part == 0 else owner
        block = g.at[own + owner, pl.ds(pl.multiple_of(half * HALF, HALF), HALF)]
        return remote(block, block, core_sem.at[0, part], core_sem.at[1, part], sibling)

    def rows_of(half, k):
        return pl.ds(pl.multiple_of(half * HALF + k * CHUNK, CHUNK), CHUNK)

    def across(first, j, k):
        block = g.at[first + j, rows_of(core, k)]
        return remote(block, block, y_sem.at[0, j, k], y_sem.at[1, j, k], partner)

    def forward(half, j, k):
        block = g.at[other + j, rows_of(half, k)]
        return remote(block, block, fwd_sem.at[0, j, k], fwd_sem.at[1, j, k], sibling)

    load_p.wait()
    share(0, core).start()
    order = [(j, k) for j in range(2) for k in range(CHUNKS)]

    @pl.when(core == 0)
    def _():
        for j, k in order[:min(DEPTH,CHUNKS)]:
            across(own, j, k).start()

    share(1, core).start()
    share(0, 1 - core).wait_recv()

    @pl.when(core == 1)
    def _():
        for j, k in order[:min(DEPTH,CHUNKS)]:
            across(own, j, k).start()

    for j, k in order[min(DEPTH,CHUNKS):DEPTH]:
        across(own, j, k).start()

    share(1, 1 - core).wait_recv()
    load_e.wait()

    def wide(rows, tile):
        if tile < 3:
            return e[rows, tile * 256 : (tile + 1) * 256]
        return jnp.concatenate([g[own, rows], g[own + 1, rows]], axis=1)

    def project(group, blocks, rows, start):
        left = jnp.concatenate([g[b, rows] for b in blocks], axis=1) if len(blocks) > 1 else g[blocks[0], rows]
        for tile in range(group.tiles // 2):
            part = tdot(left, wide(rows, tile)).reshape(NX, group.depth, 256)
            where = (slice(None), slice(None), slice(tile * 256, (tile + 1) * 256))
            if start:
                group.acc[where] = part
            else:
                group.acc[where] += part

    first, middle, last = groups
    project(first, [own, own + 1], pl.ds(0, CHUNK), True)

    @pl.loop(1, ROWS // CHUNK)
    def _(k):
        project(first, [own, own + 1], pl.ds(pl.multiple_of(k * CHUNK, CHUNK), CHUNK), False)

    first.step1()

    def arrive(j, k, group):
        across(other, j, k).wait_recv()
        n = j * CHUNKS + k + DEPTH
        if n < len(order): across(own, *order[n]).start()
        forward(core, j, k).start()
        project(group, [other + j], rows_of(core, k), k == 0)
        forward(1 - core, j, k).wait_recv()
        project(group, [other + j], rows_of(1 - core, k), False)

    C = CHUNKS
    hooks = {(0, C - 2 if C > 2 else C - 1): [first.step2], (0, C - 1): [middle.step1], (1, max(0, C - 3)): [first.step3], (1, C - 2): [first.step4, middle.step2]}
    for j in range(2):
        for k in range(C):
            arrive(j, k, (middle, last)[j])
            for h in hooks.get((j, k), []):
                h()
    last.step1()
    last.step2()
    middle.step3()
    first.step5([0, 2])
    last.step3()
    middle.step4()
    first.step5b([1])
    last.step4()
    middle.step5()
    last.step5()
    load_t.wait()
    t0_high, t0_low = split(t[0])
    t1_high, t1_low = split(t[1])
    first.step6()
    middle.step6()
    last.step6()

    def finish(p1, p2, cross, transposed):
        for n in range(3):
            lead_in = p1(n)
            lead = (dot(t0_high, lead_in) + dot(t0_low, lead_in)).astype(BF16)
            y[0:256, n * 256 : (n + 1) * 256] = lead
            pulled = tdot(cross, lead) if transposed else dot(cross, lead)
            high, low = split(p2(n).astype(F32) - pulled)
            trail = dot(t1_high, high) + dot(t1_high, low) + dot(t1_low, high)
            y[256:512, n * 256 : (n + 1) * 256] = trail.astype(BF16)

    def mine(n):
        return first.columns(2 * n, 2)

    def theirs(n):
        return jnp.concatenate([middle.columns(2 * n, 2), last.columns(2 * n, 2)], axis=0)

    @pl.when(y_lo == 0)
    def _():
        finish(mine, theirs, theirs(3), False)

    @pl.when(y_lo == 1)
    def _():
        finish(theirs, mine, theirs(3), True)

    share(0, core).wait_send()
    share(1, core).wait_send()
    for j in range(2):
        for k in range(CHUNKS):
            across(own, j, k).wait_send()
            forward(core, j, k).wait_send()
    for group in groups:
        group.drain()


BLOCK = 1024


def update(e, g, y, out):
    rows = pl.ds(pl.multiple_of(pl.program_id(0) * BLOCK, BLOCK), BLOCK)
    left = jnp.concatenate([g[b, rows] for b in range(4)], axis=1)
    for n in range(3):
        where = slice(n * 256, (n + 1) * 256)
        out[:, where] = (e[rows, where].astype(F32) - dot(left, y[:, where])).astype(BF16)


def per_device(eigvecs, panels, t_factors):
    scratch = [pltpu.VMEM((2, 256, 256), F32)]
    for size in GROUPS:
        scratch += group_scratch(*size)
    scratch += [
        pltpu.SemaphoreType.DMA((3,)),
        pltpu.SemaphoreType.DMA((2, 2)),
        pltpu.SemaphoreType.DMA((2, 2, CHUNKS)),
        pltpu.SemaphoreType.DMA((2, 2, CHUNKS)),
    ]
    hbm = pl.BlockSpec(memory_space=pltpu.HBM)
    vmem = pl.BlockSpec(memory_space=pltpu.VMEM)
    e, g, y = pl.pallas_call(
        gather_and_reduce,
        out_shape=(
            pltpu.VMEM((ROWS, COLS), BF16),
            pltpu.VMEM((4, ROWS, W), BF16),
            pltpu.VMEM((512, COLS), BF16),
        ),
        in_specs=[hbm] * 3,
        out_specs=(vmem,) * 3,
        scratch_shapes=scratch,
        compiler_params=pltpu.CompilerParams(collective_id=0, has_side_effects=True, vmem_limit_bytes=32 << 20),
        name="gather_and_reduce",
    )(*[pltpu.with_memory_space_constraint(a, pltpu.HBM) for a in (eigvecs, panels, t_factors)])
    return pl.pallas_call(
        update,
        out_shape=jax.ShapeDtypeStruct((ROWS, COLS), BF16),
        grid=(ROWS // BLOCK,),
        in_specs=[vmem] * 3,
        out_specs=pl.BlockSpec((BLOCK, COLS), lambda i: (i, 0)),
        compiler_params=pltpu.CompilerParams(vmem_limit_bytes=24 << 20),
        name="update",
    )(e, g, y)


def solution(mesh):
    in_specs = (P("row", "col"), P("row", "col"), P())
    return jax.shard_map(per_device, mesh=mesh, in_specs=in_specs, out_specs=P("row", "col"), check_vma=False)
```

```python
import jax
import jax.numpy as jnp
from jax import lax
from jax.experimental import pallas as pl
from jax.experimental.pallas import tpu as pltpu
from jax.sharding import PartitionSpec as P

MESH = pl.DeviceIdType.MESH
NX, NZ = 4, 8
ROWS = 3072
COLS = 768
W = 128
WIDE = COLS + 2 * W
HALF = ROWS // 2
CHUNKS = 3
CHUNK = HALF // CHUNKS
DEPTH = 3
GROUPS = ((64, 6), (32, 8), (32, 8))
BF16 = jnp.bfloat16
F32 = jnp.float32


def tdot(a, b):
    return lax.dot_general(a, b, (((0,), (0,)), ((), ())), preferred_element_type=F32)


def dot(a, b):
    return jnp.dot(a, b, preferred_element_type=F32)


def split(value):
    high = value.astype(BF16)
    return high, (value - high.astype(F32)).astype(BF16)


def place():
    row, col = lax.axis_index("row"), lax.axis_index("col")
    return row // 16, lax.rem(row // 2, 8), lax.rem(row, 2), col // 2, lax.rem(col, 2)


def device(x, z, y_hi, y_lo, core):
    return ((x * NZ + z) * 2 + y_hi, y_lo * 2 + core)


class Group:
    def __init__(self, depth, tiles, refs):
        self.depth, self.tiles, self.part = depth, tiles, depth * tiles // NZ
        (self.acc, self.xs, self.xr, self.zf, self.zs, self.zr, self.yf, self.yr, self.full, self.sem3, self.sem7, self.sem1) = refs

    def bind(self, x, z, y_hi, y_lo, core):
        self.x, self.z = x, z
        self.x_peer = [device(lax.rem(x + d, NX), z, y_hi, y_lo, core) for d in range(1, NX)]
        self.z_peer = [device(x, lax.rem(z + d, NZ), y_hi, y_lo, core) for d in range(1, NZ)]
        self.y_peer = device(x, z, 1 - y_hi, y_lo, core)

    def copy(self, src, dst, send, recv, peer):
        return pltpu.make_async_remote_copy(
            src_ref=src, dst_ref=dst, send_sem=send, recv_sem=recv, device_id=peer, device_id_type=MESH
        )

    def slot(self, z):
        return pl.ds(pl.multiple_of(z * self.part, 16), self.part)

    def x_reduce(self):
        return [
            self.copy(self.xs.at[lax.rem(self.x + d, NX)], self.xr.at[d - 1], self.sem3.at[0, d - 1], self.sem3.at[1, d - 1], self.x_peer[d - 1])
            for d in range(1, NX)
        ]

    def z_reduce(self):
        return [
            self.copy(self.zs.at[self.slot(lax.rem(self.z + d, NZ))], self.zr.at[d - 1], self.sem7.at[0, d - 1], self.sem7.at[1, d - 1], self.z_peer[d - 1])
            for d in range(1, NZ)
        ]

    def y_swap(self):
        return self.copy(self.yf, self.yr, self.sem1.at[0], self.sem1.at[1], self.y_peer)

    def z_gather(self, sender):
        out = []
        for d in range(1, NZ):
            block = self.full.at[self.x, self.slot(self.z if sender else lax.rem(self.z + NZ - d, NZ))]
            out.append(self.copy(block, block, self.sem7.at[2, d - 1], self.sem7.at[3, d - 1], self.z_peer[d - 1]))
        return out

    def x_gather(self, sender):
        out = []
        for d in range(1, NX):
            block = self.full.at[self.x if sender else lax.rem(self.x + NX - d, NX)]
            out.append(self.copy(block, block, self.sem3.at[2, d - 1], self.sem3.at[3, d - 1], self.x_peer[d - 1]))
        return out

    def step1(self):
        self.xs[...] = self.acc[...].astype(BF16)
        for c in self.x_reduce():
            c.start()

    def step2(self):
        for c in self.x_reduce():
            c.wait_recv()
        total = self.acc[self.x]
        for d in range(NX - 1):
            total = total + self.xr[d].astype(F32)
        for t in range(self.tiles):
            tile, where = total[:, t * W : (t + 1) * W], slice(t * self.depth, (t + 1) * self.depth)
            self.zf[where] = tile
            self.zs[where] = tile.astype(BF16)
        for c in self.z_reduce():
            c.start()

    def step3(self):
        for c in self.z_reduce():
            c.wait_recv()
        total = self.zf[self.slot(self.z)]
        for d in range(NZ - 1):
            total = total + self.zr[d].astype(F32)
        self.yf[...] = total
        self.y_swap().start()

    def step4(self):
        self.y_swap().wait_recv()
        self.full[self.x, self.slot(self.z)] = (self.yf[...] + self.yr[...]).astype(BF16)
        for c in self.z_gather(True):
            c.start()

    def step5(self, which=None):
        for c in self.z_gather(False):
            c.wait_recv()
        if which is None: which=range(NX-1)
        cs = self.x_gather(True)
        for d in which:
            cs[d].start()

    def step5b(self, which):
        cs = self.x_gather(True)
        for d in which:
            cs[d].start()

    def step6(self):
        for c in self.x_gather(False):
            c.wait_recv()

    def drain(self):
        for c in self.x_reduce() + self.z_reduce() + [self.y_swap()] + self.z_gather(True) + self.x_gather(True):
            c.wait_send()

    def columns(self, first, tiles):
        n = self.depth
        strips = [jnp.concatenate([self.full[k, t * n : (t + 1) * n] for k in range(NX)], axis=0) for t in range(first, first + tiles)]
        return jnp.concatenate(strips, axis=1)


def group_scratch(depth, tiles):
    wide, flat, part = tiles * W, tiles * depth, tiles * depth // NZ
    return [
        pltpu.VMEM((NX, depth, wide), F32),
        pltpu.VMEM((NX, depth, wide), BF16),
        pltpu.VMEM((NX - 1, depth, wide), BF16),
        pltpu.VMEM((flat, W), F32),
        pltpu.VMEM((flat, W), BF16),
        pltpu.VMEM((NZ - 1, part, W), BF16),
        pltpu.VMEM((part, W), F32),
        pltpu.VMEM((part, W), F32),
        pltpu.VMEM((NX, flat, W), BF16),
        pltpu.SemaphoreType.DMA((4, NX - 1)),
        pltpu.SemaphoreType.DMA((4, NZ - 1)),
        pltpu.SemaphoreType.DMA((2,)),
    ]


PER_GROUP = 12


def gather_and_reduce(e_hbm, p_hbm, t_hbm, e, g, y, t, *scratch):
    groups = [Group(*size, scratch[k * PER_GROUP : (k + 1) * PER_GROUP]) for k, size in enumerate(GROUPS)]
    load_sem, core_sem, y_sem, fwd_sem = scratch[len(GROUPS) * PER_GROUP :]
    x, z, y_hi, y_lo, core = place()
    for group in groups:
        group.bind(x, z, y_hi, y_lo, core)
    own, other = 2 * y_lo, 2 * (1 - y_lo)
    sibling = device(x, z, y_hi, y_lo, 1 - core)
    partner = device(x, z, y_hi, 1 - y_lo, core)

    load_p = pltpu.make_async_copy(p_hbm, g.at[own + core], load_sem.at[0])
    load_e = pltpu.make_async_copy(e_hbm, e, load_sem.at[1])
    load_t = pltpu.make_async_copy(t_hbm, t, load_sem.at[2])
    load_p.start()
    load_e.start()
    load_t.start()

    barrier = pltpu.get_barrier_semaphore()
    peers = [sibling, partner, groups[0].y_peer] + groups[0].x_peer + groups[0].z_peer
    for peer in peers:
        pl.semaphore_signal(barrier, inc=1, device_id=peer, device_id_type=MESH)
    pl.semaphore_wait(barrier, len(peers))

    def remote(src, dst, send, recv, peer):
        return pltpu.make_async_remote_copy(
            src_ref=src, dst_ref=dst, send_sem=send, recv_sem=recv, device_id=peer, device_id_type=MESH
        )

    def share(part, owner):
        half = (1 - owner) if part == 0 else owner
        block = g.at[own + owner, pl.ds(pl.multiple_of(half * HALF, HALF), HALF)]
        return remote(block, block, core_sem.at[0, part], core_sem.at[1, part], sibling)

    def rows_of(half, k):
        return pl.ds(pl.multiple_of(half * HALF + k * CHUNK, CHUNK), CHUNK)

    def across(first, j, k):
        block = g.at[first + j, rows_of(core, k)]
        return remote(block, block, y_sem.at[0, j, k], y_sem.at[1, j, k], partner)

    def forward(half, j, k):
        block = g.at[other + j, rows_of(half, k)]
        return remote(block, block, fwd_sem.at[0, j, k], fwd_sem.at[1, j, k], sibling)

    load_p.wait()
    share(0, core).start()
    order = [(j, k) for j in range(2) for k in range(CHUNKS)]

    @pl.when(core == 0)
    def _():
        for j, k in order[:min(DEPTH,CHUNKS)]:
            across(own, j, k).start()

    share(1, core).start()
    share(0, 1 - core).wait_recv()

    @pl.when(core == 1)
    def _():
        for j, k in order[:min(DEPTH,CHUNKS)]:
            across(own, j, k).start()

    for j, k in order[min(DEPTH,CHUNKS):DEPTH]:
        across(own, j, k).start()

    share(1, 1 - core).wait_recv()
    load_e.wait()

    def wide(rows, tile):
        if tile < 3:
            return e[rows, tile * 256 : (tile + 1) * 256]
        return jnp.concatenate([g[own, rows], g[own + 1, rows]], axis=1)

    def project(group, blocks, rows, start):
        left = jnp.concatenate([g[b, rows] for b in blocks], axis=1) if len(blocks) > 1 else g[blocks[0], rows]
        for tile in range(group.tiles // 2):
            part = tdot(left, wide(rows, tile)).reshape(NX, group.depth, 256)
            where = (slice(None), slice(None), slice(tile * 256, (tile + 1) * 256))
            if start:
                group.acc[where] = part
            else:
                group.acc[where] += part

    first, middle, last = groups
    project(first, [own, own + 1], pl.ds(0, CHUNK), True)

    @pl.loop(1, ROWS // CHUNK)
    def _(k):
        project(first, [own, own + 1], pl.ds(pl.multiple_of(k * CHUNK, CHUNK), CHUNK), False)

    first.step1()

    def arrive(j, k, group):
        across(other, j, k).wait_recv()
        n = j * CHUNKS + k + DEPTH
        if n < len(order): across(own, *order[n]).start()
        forward(core, j, k).start()
        project(group, [other + j], rows_of(core, k), k == 0)
        forward(1 - core, j, k).wait_recv()
        project(group, [other + j], rows_of(1 - core, k), False)

    C = CHUNKS
    hooks = {(0, C - 2 if C > 2 else C - 1): [first.step2], (0, C - 1): [middle.step1], (1, max(0, C - 3)): [first.step3], (1, C - 2): [first.step4, middle.step2]}
    for j in range(2):
        for k in range(C):
            arrive(j, k, (middle, last)[j])
            for h in hooks.get((j, k), []):
                h()
    last.step1()
    last.step2()
    middle.step3()
    first.step5([1])
    last.step3()
    middle.step4()
    first.step5b([0,2])
    last.step4()
    middle.step5([1, 0, 2])
    last.step5([1, 0, 2])
    load_t.wait()
    t0_high, t0_low = split(t[0])
    t1_high, t1_low = split(t[1])
    first.step6()
    middle.step6()
    last.step6()

    def finish(p1, p2, cross, transposed):
        for n in range(3):
            lead_in = p1(n)
            lead = (dot(t0_high, lead_in) + dot(t0_low, lead_in)).astype(BF16)
            y[0:256, n * 256 : (n + 1) * 256] = lead
            pulled = tdot(cross, lead) if transposed else dot(cross, lead)
            high, low = split(p2(n).astype(F32) - pulled)
            trail = dot(t1_high, high) + dot(t1_high, low) + dot(t1_low, high)
            y[256:512, n * 256 : (n + 1) * 256] = trail.astype(BF16)

    def mine(n):
        return first.columns(2 * n, 2)

    def theirs(n):
        return jnp.concatenate([middle.columns(2 * n, 2), last.columns(2 * n, 2)], axis=0)

    @pl.when(y_lo == 0)
    def _():
        finish(mine, theirs, theirs(3), False)

    @pl.when(y_lo == 1)
    def _():
        finish(theirs, mine, theirs(3), True)

    share(0, core).wait_send()
    share(1, core).wait_send()
    for j in range(2):
        for k in range(CHUNKS):
            across(own, j, k).wait_send()
            forward(core, j, k).wait_send()
    for group in groups:
        group.drain()


BLOCK = 1536


def update(e, g, y, out):
    rows = pl.ds(pl.multiple_of(pl.program_id(0) * BLOCK, BLOCK), BLOCK)
    left = jnp.concatenate([g[b, rows] for b in range(4)], axis=1)
    for n in range(3):
        where = slice(n * 256, (n + 1) * 256)
        out[:, where] = (e[rows, where].astype(F32) - dot(left, y[:, where])).astype(BF16)


def per_device(eigvecs, panels, t_factors):
    scratch = [pltpu.VMEM((2, 256, 256), F32)]
    for size in GROUPS:
        scratch += group_scratch(*size)
    scratch += [
        pltpu.SemaphoreType.DMA((3,)),
        pltpu.SemaphoreType.DMA((2, 2)),
        pltpu.SemaphoreType.DMA((2, 2, CHUNKS)),
        pltpu.SemaphoreType.DMA((2, 2, CHUNKS)),
    ]
    hbm = pl.BlockSpec(memory_space=pltpu.HBM)
    vmem = pl.BlockSpec(memory_space=pltpu.VMEM)
    e, g, y = pl.pallas_call(
        gather_and_reduce,
        out_shape=(
            pltpu.VMEM((ROWS, COLS), BF16),
            pltpu.VMEM((4, ROWS, W), BF16),
            pltpu.VMEM((512, COLS), BF16),
        ),
        in_specs=[hbm] * 3,
        out_specs=(vmem,) * 3,
        scratch_shapes=scratch,
        compiler_params=pltpu.CompilerParams(collective_id=0, has_side_effects=True, vmem_limit_bytes=32 << 20),
        name="gather_and_reduce",
    )(*[pltpu.with_memory_space_constraint(a, pltpu.HBM) for a in (eigvecs, panels, t_factors)])
    return pl.pallas_call(
        update,
        out_shape=jax.ShapeDtypeStruct((ROWS, COLS), BF16),
        grid=(ROWS // BLOCK,),
        in_specs=[vmem] * 3,
        out_specs=pl.BlockSpec((BLOCK, COLS), lambda i: (i, 0)),
        compiler_params=pltpu.CompilerParams(vmem_limit_bytes=24 << 20),
        name="update",
    )(e, g, y)


def solution(mesh):
    in_specs = (P("row", "col"), P("row", "col"), P())
    return jax.shard_map(per_device, mesh=mesh, in_specs=in_specs, out_specs=P("row", "col"), check_vma=False)
```
